32 devices in a mesh: groups: 2 (over x), patch: 16 (over z, y, core).
Axes of the slice: x: 2, y: 2, z: 4, core: 2. Of those that a mesh axis runs over, the one named last changes fastest.
Arguments:
- latents: bfloat16 [2816, 1280], P(('groups', 'patch')), parts along dimension 0, may hold values from -45 to 45, as said below
- stale_kv: bfloat16 [2816, 1280], P(('groups', 'patch')), parts along dimension 0, may hold values from -120 to 120
- stale_moments: float32 [32, 64], P(('groups', 'patch')), parts along dimension 0, may hold values from -1760 to 140800, as said below
- norm_gain: float32 [1280], replicated, may hold values from 0.25 to 1.75
- norm_shift: float32 [1280], replicated, may hold values from -3 to 3
- w_qkv: bfloat16 [1280, 1920], replicated, may hold values from -0.3125 to 0.3125
- w_out: bfloat16 [640, 1280], replicated, may hold values from -0.25 to 0.25
- out_bias: float32 [1280], replicated, may hold values from -2 to 2
Outputs:
- attention_out: bfloat16 [2816, 1280], P(('groups', 'patch')), parts along dimension 0
- fresh_kv: bfloat16 [2816, 1280], P(('groups', 'patch')), parts along dimension 0
The draws below stay inside these ranges and needn't reach their ends.
There are 2 independent parts, one for each index of `groups`. The reference program is written for one: setup_inputs(seed, part) draws one part's arguments, and reference() takes and returns one part's arrays. A program takes and returns all parts, laid end to end along the dimension named above; an argument that names none is the same for every part. Nothing has to cross between parts.
Inputs may be any that keep to these rules, and one draw needn't show every extreme that they name: `latents`: channels have scales of their own and tokens too. `stale_moments`: each row holds for every group the sum of values and the sum of their squares over 3520 elements.
All inputs are finite; a program needn't handle non-finite values.
Results may differ from the reference program's by a relative error of at most 0.0065.
The reference program's roundings to bfloat16 on the way count: a program that leaves them out, or rounds other values in their place, can miss the bound.
Values may be sent and summed in bfloat16 or wider, within the bound.
A program may use at most 128 MiB of HBM per device.

```python
import math
import jax
import jax.numpy as jnp
from jax import lax

D = 1280
HEADS = 10
HDIM = 64
GROUPS = 32
TOK_DEV = 88
TOKENS = 1408
N_PATCH = 16


def draw_latents(key, part):
    key = jax.random.fold_in(key, 11)
    first_key, second_key, third_key = jax.random.split(key, 3)
    channel_scale = jnp.exp(jax.random.uniform(first_key, (D,), jnp.float32, math.log(0.4), math.log(4.0)))
    token_scale = jnp.exp(jax.random.uniform(second_key, (TOKENS, 1), jnp.float32, math.log(0.6), math.log(1.7)))
    base_values = jnp.clip(jax.random.normal(third_key, (TOKENS, D), jnp.float32), -5.0, 5.0)
    return (base_values * channel_scale * token_scale).astype(jnp.bfloat16)


def draw_stale_kv(key, part):
    key = jax.random.fold_in(key, 12)
    first_key = jax.random.fold_in(key, 0)
    inner_width = HEADS * HDIM
    base_values = 1.7 * jnp.clip(jax.random.normal(first_key, (TOKENS, 2 * inner_width), jnp.float32), -5.0, 5.0)
    return base_values.astype(jnp.bfloat16)


def draw_stale_moments(key, part):
    key = jax.random.fold_in(key, 13)
    first_key, second_key = jax.random.split(key, 2)
    element_count = float(TOK_DEV * (D // GROUPS))
    rise = 1.0 + 2.0 * jnp.arange(N_PATCH, dtype=jnp.float32) / max(N_PATCH - 1, 1)
    group_mean = jax.random.uniform(first_key, (N_PATCH, GROUPS), jnp.float32, -0.5, 0.5)
    spread = jnp.exp(jax.random.uniform(second_key, (N_PATCH, GROUPS), jnp.float32, math.log(0.5), math.log(5.0)))
    second_sums = (group_mean * group_mean + spread * rise[:, None]) * element_count
    first_sums = group_mean * element_count
    return jnp.concatenate([first_sums, second_sums], axis=1).astype(jnp.float32)


def gaussian(own_key, shape, width, bound, held_as=jnp.bfloat16):
    return jnp.clip(width * jax.random.normal(own_key, shape, jnp.float32), -bound, bound).astype(held_as)


def setup_inputs(seed: int = 0, part: int = 0) -> dict:
    key_list = jax.random.split(jax.random.key(seed), 9)
    part_keys = jax.random.split(jax.random.fold_in(key_list[8], part), 9)
    latents = draw_latents(jax.random.fold_in(jax.random.fold_in(key_list[8], part), 71), part)
    stale_kv = draw_stale_kv(jax.random.fold_in(jax.random.fold_in(key_list[8], part), 71), part)
    stale_moments = draw_stale_moments(jax.random.fold_in(jax.random.fold_in(key_list[8], part), 71), part)
    norm_gain = jnp.clip(1.0 + 0.15 * jax.random.normal(key_list[3], (D,), jnp.float32), 0.25, 1.75)
    norm_shift = gaussian(key_list[4], (D,), 0.5, 3.0, jnp.float32)
    w_qkv = gaussian(key_list[5], (D, 3 * HEADS * HDIM), (D // 3) ** -0.5, 0.3125)
    w_out = gaussian(key_list[6], (HEADS * HDIM, D), (HEADS * HDIM) ** -0.5, 0.25)
    out_bias = gaussian(key_list[7], (D,), 0.3, 2.0, jnp.float32)
    return {"latents": latents, "stale_kv": stale_kv, "stale_moments": stale_moments, "norm_gain": norm_gain, "norm_shift": norm_shift, "w_qkv": w_qkv, "w_out": w_out, "out_bias": out_bias}


def reference(latents, stale_kv, stale_moments, norm_gain, norm_shift, w_qkv, w_out, out_bias):
    token_count, feature_width = latents.shape
    strips = stale_moments.shape[0]
    row_count = token_count // strips
    group_size = feature_width // GROUPS
    grouped = latents.astype(jnp.float32).reshape(strips, row_count, GROUPS, group_size)
    fresh_moments = jnp.concatenate([lax.optimization_barrier(jnp.sum(grouped, axis=(1, 3))), lax.optimization_barrier(jnp.sum(grouped * grouped, axis=(1, 3)))], axis=1)
    totals = fresh_moments + (lax.optimization_barrier(jnp.sum(stale_moments, axis=0))[None, :] - stale_moments)
    element_count = float(token_count * group_size)
    group_mean = totals[:, :GROUPS] / element_count
    spread = totals[:, GROUPS:] / element_count - group_mean * group_mean
    inverse_std = lax.rsqrt(spread + 1e-06)
    normed = ((grouped - group_mean[:, None, :, None]) * inverse_std[:, None, :, None]).reshape(token_count, feature_width)
    normed = (normed * norm_gain + norm_shift).astype(jnp.bfloat16)
    projected = jnp.dot(normed, w_qkv, preferred_element_type=jnp.float32).astype(jnp.bfloat16)
    inner_width = HEADS * HDIM
    fresh_kv = projected[:, inner_width:]
    queries = projected[:, :inner_width].astype(jnp.float32).reshape(strips, row_count, HEADS, HDIM)
    stale_keys = stale_kv[:, :inner_width].astype(jnp.float32).reshape(token_count, HEADS, HDIM)
    stale_values = stale_kv[:, inner_width:].astype(jnp.float32).reshape(token_count, HEADS, HDIM)
    fresh_pairs = fresh_kv.astype(jnp.float32).reshape(strips, row_count, 2, HEADS, HDIM)
    owners = jnp.arange(token_count, dtype=jnp.int32) // row_count

    def one_strip(strip):
        own_queries = queries[strip]
        own_pairs = fresh_pairs[strip]
        near = jnp.einsum('qhd,khd->hqk', own_queries, own_pairs[:, 0]) * 0.125
        far = jnp.einsum('qhd,khd->hqk', own_queries, stale_keys) * 0.125
        far = jnp.where((owners != strip)[None, None, :], far, -1e+30)
        highest = jnp.maximum(lax.optimization_barrier(jnp.max(near, axis=-1)), lax.optimization_barrier(jnp.max(far, axis=-1)))[:, :, None]
        near_weights = jnp.exp(near - highest)
        far_weights = jnp.exp(far - highest)
        total_mass = lax.optimization_barrier(jnp.sum(near_weights, axis=-1)) + lax.optimization_barrier(jnp.sum(far_weights, axis=-1))
        near_rounded = lax.optimization_barrier(near_weights.astype(jnp.bfloat16)).astype(jnp.float32)
        far_rounded = lax.optimization_barrier(far_weights.astype(jnp.bfloat16)).astype(jnp.float32)
        weighted = jnp.einsum('hqk,khd->qhd', near_rounded, own_pairs[:, 1])
        weighted = weighted + jnp.einsum('hqk,khd->qhd', far_rounded, stale_values)
        return weighted / jnp.transpose(total_mass)[:, :, None]
    attended = lax.map(one_strip, jnp.arange(strips, dtype=jnp.int32))
    attended = attended.reshape(token_count, inner_width).astype(jnp.bfloat16)
    result = (jnp.dot(attended, w_out, preferred_element_type=jnp.float32) + out_bias).astype(jnp.bfloat16)
    return (result, fresh_kv)
```

```python
import functools

import jax
import jax.numpy as jnp
from jax import lax
from jax.experimental import pallas as pl
from jax.experimental.pallas import tpu as pltpu
from jax.sharding import PartitionSpec as P

MESH = pl.DeviceIdType.MESH
PAIR = 128
QUAD = 4
WAYS = 4
NEG = -1e30
F32 = jnp.float32
BF16 = jnp.bfloat16


def dot_t(a, b):
    return lax.dot_general(a, b, (((1,), (1,)), ((), ())), preferred_element_type=F32)


def thirds(row):
    high = row.astype(BF16).astype(F32)
    rest = row - high
    mid = rest.astype(BF16).astype(F32)
    return high, mid, rest - mid


def kernel(
    n, rows, pad,
    x_ref, stale_ref, mom_ref, gain_ref, shift_ref, wqkv_ref, wout_ref, bias_ref,
    out_ref, fresh_ref,
    sb, kv, momb, qs, qb, ob, og, wq, wo,
    mom_send, mom_recv, kv_send, kv_recv, core_send, side_send,
    q_send, q_recv, o_send, o_recv, w_sem,
):
    width = x_ref.shape[1]
    inner = stale_ref.shape[1] // 2
    me = lax.axis_index("patch")
    quad = lax.rem(me, QUAD)
    row = me // QUAD
    way = lax.rem(row, WAYS)
    block = row // WAYS
    lines = n // QUAD
    blocks = lines // WAYS

    weight_copies = [
        pltpu.make_async_copy(
            wqkv_ref.at[:, pl.ds(i * inner, inner)], wq.at[i], w_sem.at[i]
        )
        for i in range(3)
    ]
    out_copy = pltpu.make_async_copy(wout_ref, wo, w_sem.at[3])
    for copy in weight_copies:
        copy.start()
    out_copy.start()

    barrier = pltpu.get_barrier_semaphore()

    def greet(i, carry):
        pl.semaphore_signal(
            barrier, inc=1, device_id={"patch": lax.rem(me + 1 + i, n)}, device_id_type=MESH
        )
        return carry

    lax.fori_loop(0, n - 1, greet, 0, unroll=True)

    momb[me] = jnp.broadcast_to(mom_ref[...], (8, mom_ref.shape[1]))
    tail = jnp.zeros((pad - rows, PAIR), F32)

    def piece(c):
        part = stale_ref[:, c * PAIR:(c + 1) * PAIR].astype(F32)
        return jnp.concatenate([part, tail], axis=0).astype(BF16)

    pairs = inner // PAIR
    for w in range(WAYS):
        sb[w, 0] = piece(w)
        sb[w, 1] = piece(pairs + w)
        sb[w, 2] = piece(WAYS)
        sb[w, 3] = piece(pairs + WAYS)
    kv[me] = sb[way]

    pl.semaphore_wait(barrier, n - 1)

    def mom_copy(i):
        peer = lax.rem(me + 1 + i, n)
        return pltpu.make_async_remote_copy(
            src_ref=momb.at[me], dst_ref=momb.at[me],
            send_sem=mom_send.at[i], recv_sem=mom_recv.at[me],
            device_id={"patch": peer}, device_id_type=MESH,
        )

    def mom_wait(i):
        peer = lax.rem(me + 1 + i, n)
        return pltpu.make_async_remote_copy(
            src_ref=momb.at[peer], dst_ref=momb.at[peer],
            send_sem=mom_send.at[i], recv_sem=mom_recv.at[peer],
            device_id={"patch": peer}, device_id_type=MESH,
        )

    def line_row(k):
        return lax.rem(row + k, lines)

    def line_copy(k):
        peer_row = line_row(k)
        return pltpu.make_async_remote_copy(
            src_ref=sb.at[lax.rem(peer_row, WAYS)], dst_ref=kv.at[me],
            send_sem=kv_send.at[k], recv_sem=kv_recv.at[me],
            device_id={"patch": peer_row * QUAD + quad}, device_id_type=MESH,
        )

    core_quad = quad + 1 - 2 * lax.rem(quad, 2)
    side_quad = lax.rem(quad + 2, QUAD)
    far_quad = lax.rem(core_quad + 2, QUAD)

    def slot_copy(slot, sems, to_quad):
        return pltpu.make_async_remote_copy(
            src_ref=kv.at[slot], dst_ref=kv.at[slot],
            send_sem=sems.at[slot], recv_sem=kv_recv.at[slot],
            device_id={"patch": row * QUAD + to_quad}, device_id_type=MESH,
        )

    def pair_copy(k, src, dst, send, recv):
        peer_way = lax.rem(way + k, WAYS)
        return pltpu.make_async_remote_copy(
            src_ref=src.at[peer_way], dst_ref=dst.at[way],
            send_sem=send.at[k], recv_sem=recv.at[way],
            device_id={"patch": (block * WAYS + peer_way) * QUAD + quad},
            device_id_type=MESH,
        )

    def pair_wait(k, src, dst, send, recv):
        peer_way = lax.rem(way + k, WAYS)
        return pltpu.make_async_remote_copy(
            src_ref=dst.at[peer_way], dst_ref=dst.at[peer_way],
            send_sem=send.at[k], recv_sem=recv.at[peer_way],
            device_id={"patch": (block * WAYS + peer_way) * QUAD + quad},
            device_id_type=MESH,
        )

    for i in range(n - 1):
        mom_copy(i).start()
    for k in range(1, lines):
        line_copy(k).start()
    slot_copy(me, side_send, side_quad).start()
    slot_copy(me, core_send, core_quad).start()

    count = mom_ref.shape[1]
    groups = count // 2
    size = width // groups
    x = x_ref[...].astype(F32)
    first = jnp.sum(x, axis=0, keepdims=True)
    second = jnp.sum(x * x, axis=0, keepdims=True)
    lane = lax.broadcasted_iota(jnp.int32, (PAIR, width), 1)
    low = lax.rem(lax.broadcasted_iota(jnp.int32, (PAIR, width), 0), groups) * size
    member = jnp.where((lane >= low) & (lane < low + size), 1.0, 0.0).astype(BF16)
    zero = jnp.zeros((1, width), F32)
    table = jnp.concatenate([*thirds(first), *thirds(second), zero, zero], axis=0)
    sums = dot_t(table.astype(BF16), member)
    head = lax.broadcasted_iota(jnp.int32, (1, PAIR), 1)
    fresh_moments = jnp.where(
        head < groups, sums[0:1] + sums[1:2] + sums[2:3], sums[3:4] + sums[4:5] + sums[5:6]
    )
    stale_sum = jnp.zeros((8, count), F32)
    for i in range(n - 1):
        mom_wait(i).wait_recv()
        stale_sum = stale_sum + momb[lax.rem(me + 1 + i, n)]
    stale_row = jnp.concatenate(
        [stale_sum[0:1], jnp.zeros((1, PAIR - count), F32)], axis=1
    )
    totals = fresh_moments + stale_row
    left = jnp.where(head < groups, totals, 0.0)
    right = jnp.where((head >= groups) & (head < count), totals, 0.0)
    none = jnp.zeros((1, PAIR), F32)
    table = jnp.concatenate([*thirds(left), *thirds(right), none, none], axis=0)
    spreadout = jnp.dot(table.astype(BF16), member, preferred_element_type=F32)
    element_count = float(n * rows * size)
    mean = (spreadout[0:1] + spreadout[1:2] + spreadout[2:3]) / element_count
    spread = (spreadout[3:4] + spreadout[4:5] + spreadout[5:6]) / element_count - mean * mean
    inverse = lax.rsqrt(spread + 1e-06)
    normed = ((x - mean) * inverse) * gain_ref[...] + shift_ref[...]
    normed = jnp.concatenate([normed, jnp.zeros((pad - rows, width), F32)], axis=0).astype(BF16)

    weight_copies[0].wait()
    queries = jnp.dot(normed, wq[0], preferred_element_type=F32).astype(BF16)
    queries = (queries.astype(F32) * 0.125).astype(BF16)
    for w in range(WAYS):
        qs[w] = queries[:, w * PAIR:(w + 1) * PAIR]
    qb[way] = qs[way]
    for k in range(1, WAYS):
        pair_copy(k, qs, qb, q_send, q_recv).start()

    def forward(k):
        slot = line_row(k) * QUAD + quad
        slot_copy(slot, side_send, side_quad).wait_recv()
        slot_copy(slot, side_send, side_quad).start()
        slot_copy(slot, core_send, core_quad).start()

    order = [1, lines - 1] + list(range(2, lines - 1))
    forward(order[0])
    weight_copies[1].wait()
    keys = jnp.dot(normed, wq[1], preferred_element_type=F32).astype(BF16)
    fresh_ref[:, :inner] = keys[:rows]
    forward(order[1])
    weight_copies[2].wait()
    values = jnp.dot(normed, wq[2], preferred_element_type=F32).astype(BF16)
    fresh_ref[:, inner:] = values[:rows]
    for k in order[2:]:
        forward(k)

    half = lax.broadcasted_iota(jnp.int32, (1, PAIR), 1) < PAIR // 2

    def one_head(query, key, value, biases):
        scores = dot_t(query, key)
        if len(biases) == 1:
            scores = scores + biases[0]
        else:
            scores = jnp.concatenate(
                [scores[i * pad:(i + 1) * pad] + b for i, b in enumerate(biases)], axis=0
            )
        top = jnp.max(scores, axis=1, keepdims=True)
        chances = jnp.exp(scores - top)
        mass = jnp.sum(chances, axis=1, keepdims=True)
        weighted = jnp.dot(chances.astype(BF16), value, preferred_element_type=F32)
        return top + jnp.log(mass), weighted / mass

    def attend(query, key, value, biases):
        none = jnp.zeros_like(query)
        lse0, out0 = one_head(jnp.where(half, query, none), key, value, biases)
        lse1, out1 = one_head(jnp.where(half, none, query), key, value, biases)
        return jnp.where(half, lse0, lse1), jnp.where(half, out0, out1)

    def merge(a, b):
        top = jnp.maximum(a[0], b[0])
        wa = jnp.exp(a[0] - top)
        wb = jnp.exp(b[0] - top)
        mass = wa + wb
        return top + jnp.log(mass), (wa * a[1] + wb * b[1]) / mass

    key_lane = lax.broadcasted_iota(jnp.int32, (1, pad), 1)
    own_bias = jnp.where(key_lane < rows, 0.0, NEG)
    fresh = []
    for p in range(pairs):
        cut = slice(p * PAIR, (p + 1) * PAIR)
        fresh.append(attend(queries[:, cut], keys[:, cut], values[:, cut], [own_bias]))

    for k in range(lines):
        slot = line_row(k) * QUAD + side_quad
        slot_copy(slot, side_send, side_quad).wait_recv()
        slot_copy(slot, core_send, core_quad).start()
    for k in range(lines):
        slot_copy(line_row(k) * QUAD + core_quad, core_send, core_quad).wait_recv()
    for k in range(lines):
        slot_copy(line_row(k) * QUAD + far_quad, core_send, core_quad).wait_recv()
    for k in range(1, WAYS):
        pair_wait(k, qs, qb, q_send, q_recv).wait_recv()

    step = n // blocks
    span = step * pad
    position = lax.broadcasted_iota(jnp.int32, (1, span), 1)
    padding = jnp.where(lax.rem(position, pad) < rows, 0.0, NEG)

    def bias_for(owner, b):
        start = (owner - b * step) * pad
        return jnp.where((position >= start) & (position < start + pad), NEG, padding)

    def stale_part(query, part, owners):
        def one(b):
            key = kv[pl.ds(b * step, step), part].reshape(span, PAIR)
            value = kv[pl.ds(b * step, step), part + 1].reshape(span, PAIR)
            return attend(query, key, value, [bias_for(o, b) for o in owners])

        state = one(0)
        if blocks > 1:
            state = lax.fori_loop(1, blocks, lambda b, s: merge(s, one(b)), state)
        return state

    owners = [(block * WAYS + w) * QUAD + quad for w in range(WAYS)]
    all_queries = qb[...].reshape(WAYS * pad, PAIR)
    lse, part = stale_part(all_queries, 0, owners)
    for w in range(WAYS):
        cut = slice(w * pad, (w + 1) * pad)
        flat = jnp.transpose(
            jnp.concatenate([lse[cut], jnp.zeros((PAIR - pad, PAIR), F32)], axis=0)
        )
        none = jnp.zeros((1, PAIR), F32)
        stats = jnp.concatenate(
            [*thirds(flat[0:1]), *thirds(flat[PAIR // 2:PAIR // 2 + 1]), none, none], axis=0
        )
        og[w] = jnp.concatenate([part[cut][:rows], stats], axis=0).astype(BF16)
    for k in range(1, WAYS):
        pair_copy(k, og, ob, o_send, o_recv).start()
    ob[way] = og[way]

    last = merge(fresh[WAYS], stale_part(queries[:, WAYS * PAIR:], 2, [me]))[1]

    for k in range(1, WAYS):
        pair_wait(k, og, ob, o_send, o_recv).wait_recv()
    heads = []
    for p in range(WAYS):
        got = ob[p].astype(F32)
        stats = got[rows:pad]
        lse0 = stats[0:1] + stats[1:2] + stats[2:3]
        lse1 = stats[3:4] + stats[4:5] + stats[5:6]
        flat = jnp.transpose(
            jnp.concatenate(
                [jnp.broadcast_to(lse0, (PAIR // 2, PAIR)), jnp.broadcast_to(lse1, (PAIR // 2, PAIR))],
                axis=0,
            )
        )[:pad]
        heads.append(merge(fresh[p], (flat, got))[1].astype(BF16))
    heads.append(last.astype(BF16))
    attended = jnp.concatenate(heads, axis=1)
    out_copy.wait()
    result = jnp.dot(attended, wo[...], preferred_element_type=F32) + bias_ref[...]
    out_ref[...] = result.astype(BF16)[:rows]

    for i in range(n - 1):
        mom_copy(i).wait_send()
    for k in range(1, lines):
        line_copy(k).wait_send()
    for k in range(lines):
        slot = line_row(k) * QUAD + quad
        slot_copy(slot, side_send, side_quad).wait_send()
        slot_copy(slot, core_send, core_quad).wait_send()
        slot = line_row(k) * QUAD + side_quad
        slot_copy(slot, core_send, core_quad).wait_send()
    for k in range(1, WAYS):
        pair_copy(k, qs, qb, q_send, q_recv).wait_send()
        pair_copy(k, og, ob, o_send, o_recv).wait_send()


def solution(mesh):
    n = mesh.shape["patch"]

    def local(latents, stale_kv, stale_moments, norm_gain, norm_shift, w_qkv, w_out, out_bias):
        rows, width = latents.shape
        inner = w_out.shape[0]
        pad = -(-rows // 16) * 16
        vmem = pl.BlockSpec(memory_space=pltpu.VMEM)
        hbm = pl.BlockSpec(memory_space=pl.ANY)
        dma = pltpu.SemaphoreType.DMA
        return pl.pallas_call(
            functools.partial(kernel, n, rows, pad),
            out_shape=(
                jax.ShapeDtypeStruct((rows, w_out.shape[1]), BF16),
                jax.ShapeDtypeStruct((rows, 2 * inner), BF16),
            ),
            in_specs=[vmem, vmem, vmem, vmem, vmem, hbm, hbm, vmem],
            out_specs=(vmem, vmem),
            scratch_shapes=[
                pltpu.VMEM((WAYS, 4, pad, PAIR), BF16),
                pltpu.VMEM((n, 4, pad, PAIR), BF16),
                pltpu.VMEM((n, 8, stale_moments.shape[1]), F32),
                pltpu.VMEM((WAYS, pad, PAIR), BF16),
                pltpu.VMEM((WAYS, pad, PAIR), BF16),
                pltpu.VMEM((WAYS, pad, PAIR), BF16),
                pltpu.VMEM((WAYS, pad, PAIR), BF16),
                pltpu.VMEM((3, width, inner), BF16),
                pltpu.VMEM(w_out.shape, BF16),
                dma((n,)), dma((n,)), dma((n // QUAD,)), dma((n,)), dma((n,)), dma((n,)),
                dma((WAYS,)), dma((WAYS,)), dma((WAYS,)), dma((WAYS,)), dma((4,)),
            ],
            compiler_params=pltpu.CompilerParams(
                collective_id=0, has_side_effects=True, vmem_limit_bytes=52 * 1024 * 1024
            ),
        )(
            latents, stale_kv, stale_moments, norm_gain[None], norm_shift[None],
            w_qkv, w_out, out_bias[None],
        )

    strip = P(("groups", "patch"), None)
    return jax.shard_map(
        local,
        mesh=mesh,
        in_specs=(strip, strip, strip, P(), P(), P(), P(), P()),
        out_specs=(strip, strip),
        check_vma=False,
    )
```

```python
import functools

import jax
import jax.numpy as jnp
from jax import lax
from jax.experimental import pallas as pl
from jax.experimental.pallas import tpu as pltpu
from jax.sharding import PartitionSpec as P

MESH = pl.DeviceIdType.MESH
PAIR = 128
CORES = 2
WAYS = 8
HOSTS = (2, 5)
NEG = -1e30
F32 = jnp.float32
BF16 = jnp.bfloat16


def dot_t(a, b):
    return lax.dot_general(a, b, (((1,), (1,)), ((), ())), preferred_element_type=F32)


def thirds(row):
    high = row.astype(BF16).astype(F32)
    rest = row - high
    mid = rest.astype(BF16).astype(F32)
    return high, mid, rest - mid


def kernel(
    n, rows, pad,
    x_hbm, stale_hbm, mom_hbm, gain_hbm, shift_hbm, wqkv_ref, wout_ref, bias_hbm,
    out_ref, fresh_ref,
    x_ref, stale_ref, mom_ref, gain_ref, shift_ref, bias_ref,
    sb, kv, kx, momb, qs, qb, qx, ob, og, ox, wq, wo,
    mom_send, mom_recv, kv_send, kv_recv, kx_send, kx_recv, core_send, corex_send,
    q_send, q_recv, qx_send, qx_recv, o_send, o_recv, ox_send, w_sem, in_sem,
):
    width = x_ref.shape[1]
    inner = stale_ref.shape[1] // 2
    me = lax.axis_index("patch")
    core = lax.rem(me, CORES)
    chip = me // CORES
    way = lax.rem(chip, WAYS)
    block = chip // WAYS
    lines = n // CORES
    blocks = lines // WAYS
    fold = pad // 2
    half = lax.broadcasted_iota(jnp.int32, (1, PAIR), 1) < PAIR // 2
    is_host = (way == HOSTS[0]) | (way == HOSTS[1])
    extra = jnp.where(way == HOSTS[1], WAYS + 1, WAYS)

    def swap(a):
        return pltpu.roll(a, PAIR // 2, 1)

    ins = [
        pltpu.make_async_copy(src, dst, in_sem.at[i])
        for i, (src, dst) in enumerate([
            (stale_hbm, stale_ref), (mom_hbm, mom_ref), (x_hbm, x_ref),
            (gain_hbm, gain_ref), (shift_hbm, shift_ref), (bias_hbm, bias_ref),
        ])
    ]
    for copy in ins:
        copy.start()
    weight_copies = [
        pltpu.make_async_copy(
            wqkv_ref.at[:, pl.ds(i * inner, inner)], wq.at[i], w_sem.at[i]
        )
        for i in range(3)
    ]
    out_copy = pltpu.make_async_copy(wout_ref, wo, w_sem.at[3])
    for copy in weight_copies:
        copy.start()
    out_copy.start()

    barrier = pltpu.get_barrier_semaphore()

    def greet(i, carry):
        pl.semaphore_signal(
            barrier, inc=1, device_id={"patch": lax.rem(me + 1 + i, n)}, device_id_type=MESH
        )
        return carry

    lax.fori_loop(0, n - 1, greet, 0, unroll=True)

    ins[0].wait()
    ins[1].wait()

    momb[me] = jnp.broadcast_to(mom_ref[...], (8, mom_ref.shape[1]))
    tail = jnp.zeros((pad - rows, PAIR), F32)

    def piece(c):
        part = stale_ref[:, c * PAIR:(c + 1) * PAIR].astype(F32)
        return jnp.concatenate([part, tail], axis=0)

    pairs = inner // PAIR
    for p in range(pairs):
        key, value = piece(p), piece(pairs + p)
        sb[2 * p] = jnp.where(half, key, swap(value)).astype(BF16)
        sb[2 * p + 1] = jnp.where(half, swap(key), value).astype(BF16)
    kv[me] = sb[way]

    @pl.when(is_host)
    def _():
        kx[me] = sb[extra]

    pl.semaphore_wait(barrier, n - 1)

    def mom_copy(i):
        peer = lax.rem(me + 1 + i, n)
        return pltpu.make_async_remote_copy(
            src_ref=momb.at[me], dst_ref=momb.at[me],
            send_sem=mom_send.at[i], recv_sem=mom_recv.at[me],
            device_id={"patch": peer}, device_id_type=MESH,
        )

    def mom_wait(i):
        peer = lax.rem(me + 1 + i, n)
        return pltpu.make_async_remote_copy(
            src_ref=momb.at[peer], dst_ref=momb.at[peer],
            send_sem=mom_send.at[i], recv_sem=mom_recv.at[peer],
            device_id={"patch": peer}, device_id_type=MESH,
        )

    def chip_at(k):
        return lax.rem(chip + k, lines)

    def line_copy(k):
        peer = chip_at(k)
        return pltpu.make_async_remote_copy(
            src_ref=sb.at[lax.rem(peer, WAYS)], dst_ref=kv.at[me],
            send_sem=kv_send.at[k], recv_sem=kv_recv.at[me],
            device_id={"patch": peer * CORES + core}, device_id_type=MESH,
        )

    def host_copy(e, b):
        peer = b * WAYS + HOSTS[e]
        return pltpu.make_async_remote_copy(
            src_ref=sb.at[WAYS + e], dst_ref=kx.at[me],
            send_sem=kx_send.at[e * blocks + b], recv_sem=kx_recv.at[me],
            device_id={"patch": peer * CORES + core}, device_id_type=MESH,
        )

    def core_copy(buf, slot, send, recv):
        return pltpu.make_async_remote_copy(
            src_ref=buf.at[slot], dst_ref=buf.at[slot],
            send_sem=send.at[slot], recv_sem=recv.at[slot],
            device_id={"patch": chip * CORES + 1 - core}, device_id_type=MESH,
        )

    def block_peer(w):
        return {"patch": (block * WAYS + w) * CORES + core}

    def way_copy(k, src, dst, send, recv):
        peer = lax.rem(way + k, WAYS)
        return pltpu.make_async_remote_copy(
            src_ref=src.at[peer], dst_ref=dst.at[way],
            send_sem=send.at[k], recv_sem=recv.at[way],
            device_id=block_peer(peer), device_id_type=MESH,
        )

    def way_wait(k, dst, send, recv):
        peer = lax.rem(way + k, WAYS)
        return pltpu.make_async_remote_copy(
            src_ref=dst.at[peer], dst_ref=dst.at[peer],
            send_sem=send.at[k], recv_sem=recv.at[peer],
            device_id=block_peer(peer), device_id_type=MESH,
        )

    def host_query(e):
        return pltpu.make_async_remote_copy(
            src_ref=qs.at[WAYS + e], dst_ref=qx.at[way],
            send_sem=qx_send.at[e], recv_sem=qx_recv.at[way],
            device_id=block_peer(HOSTS[e]), device_id_type=MESH,
        )

    def host_result(k):
        peer = lax.rem(way + k, WAYS)
        return pltpu.make_async_remote_copy(
            src_ref=ox.at[peer], dst_ref=ob.at[extra],
            send_sem=ox_send.at[k], recv_sem=o_recv.at[extra],
            device_id=block_peer(peer), device_id_type=MESH,
        )

    def host_result_wait(e):
        return pltpu.make_async_remote_copy(
            src_ref=ob.at[WAYS + e], dst_ref=ob.at[WAYS + e],
            send_sem=ox_send.at[0], recv_sem=o_recv.at[WAYS + e],
            device_id=block_peer(HOSTS[e]), device_id_type=MESH,
        )

    for i in range(n - 1):
        mom_copy(i).start()
    for e in range(2):
        for b in range(blocks):
            @pl.when(chip != b * WAYS + HOSTS[e])
            def _():
                host_copy(e, b).start()
    for k in range(1, lines):
        line_copy(k).start()
    core_copy(kv, me, core_send, kv_recv).start()

    @pl.when(is_host)
    def _():
        core_copy(kx, me, corex_send, kx_recv).start()

    count = mom_ref.shape[1]
    groups = count // 2
    size = width // groups
    for copy in ins[2:]:
        copy.wait()
    x = x_ref[...].astype(F32)
    first = jnp.sum(x, axis=0, keepdims=True)
    second = jnp.sum(x * x, axis=0, keepdims=True)
    lane = lax.broadcasted_iota(jnp.int32, (PAIR, width), 1)
    low = lax.rem(lax.broadcasted_iota(jnp.int32, (PAIR, width), 0), groups) * size
    member = jnp.where((lane >= low) & (lane < low + size), 1.0, 0.0).astype(BF16)
    zero = jnp.zeros((1, width), F32)
    table = jnp.concatenate([*thirds(first), *thirds(second), zero, zero], axis=0)
    sums = dot_t(table.astype(BF16), member)
    head = lax.broadcasted_iota(jnp.int32, (1, PAIR), 1)
    fresh_moments = jnp.where(
        head < groups, sums[0:1] + sums[1:2] + sums[2:3], sums[3:4] + sums[4:5] + sums[5:6]
    )
    stale_sum = jnp.zeros((8, count), F32)
    for i in range(n - 1):
        mom_wait(i).wait_recv()
        stale_sum = stale_sum + momb[lax.rem(me + 1 + i, n)]
    stale_row = jnp.concatenate(
        [stale_sum[0:1], jnp.zeros((1, PAIR - count), F32)], axis=1
    )
    totals = fresh_moments + stale_row
    left = jnp.where(head < groups, totals, 0.0)
    right = jnp.where((head >= groups) & (head < count), totals, 0.0)
    none = jnp.zeros((1, PAIR), F32)
    table = jnp.concatenate([*thirds(left), *thirds(right), none, none], axis=0)
    spreadout = jnp.dot(table.astype(BF16), member, preferred_element_type=F32)
    element_count = float(n * rows * size)
    mean = (spreadout[0:1] + spreadout[1:2] + spreadout[2:3]) / element_count
    spread = (spreadout[3:4] + spreadout[4:5] + spreadout[5:6]) / element_count - mean * mean
    inverse = lax.rsqrt(spread + 1e-06)
    normed = ((x - mean) * inverse) * gain_ref[...][None] + shift_ref[...][None]
    normed = jnp.concatenate([normed, jnp.zeros((pad - rows, width), F32)], axis=0).astype(BF16)

    weight_copies[0].wait()
    queries = jnp.dot(normed, wq[0], preferred_element_type=F32).astype(BF16)
    queries = (queries.astype(F32) * 0.125).astype(BF16)
    def folded(a):
        return jnp.where(half, a[:fold], swap(a[fold:]))

    for p in range(pairs):
        query = queries[:, p * PAIR:(p + 1) * PAIR].astype(F32)
        qs[2 * p] = folded(query).astype(BF16)
        qs[2 * p + 1] = folded(swap(query)).astype(BF16)
    qb[way] = qs[way]
    for k in range(1, WAYS):
        way_copy(k, qs, qb, q_send, q_recv).start()
    for e in range(2):
        @pl.when(way == HOSTS[e])
        def _():
            qx[way] = qs[WAYS + e]

        @pl.when(way != HOSTS[e])
        def _():
            host_query(e).start()

    weight_copies[1].wait()
    keys = jnp.dot(normed, wq[1], preferred_element_type=F32).astype(BF16)
    fresh_ref[:, :inner] = keys[:rows]
    weight_copies[2].wait()
    values = jnp.dot(normed, wq[2], preferred_element_type=F32).astype(BF16)
    fresh_ref[:, inner:] = values[:rows]

    def one_head(query, key, value, biases, seg):
        scores = dot_t(query, key)
        if len(biases) == 1:
            scores = scores + biases[0]
        else:
            scores = jnp.concatenate(
                [scores[i * seg:(i + 1) * seg] + b for i, b in enumerate(biases)], axis=0
            )
        top = jnp.max(scores, axis=1, keepdims=True)
        chances = jnp.exp(scores - top)
        mass = jnp.sum(chances, axis=1, keepdims=True)
        weighted = jnp.dot(chances.astype(BF16), value, preferred_element_type=F32)
        return top + jnp.log(mass), weighted / mass

    def attend(query, key, value, biases):
        none = jnp.zeros_like(query)
        lse0, out0 = one_head(jnp.where(half, query, none), key, value, biases, pad)
        lse1, out1 = one_head(jnp.where(half, none, query), key, value, biases, pad)
        return jnp.where(half, lse0, lse1), jnp.where(half, out0, out1)

    def merge(a, b):
        top = jnp.maximum(a[0], b[0])
        wa = jnp.exp(a[0] - top)
        wb = jnp.exp(b[0] - top)
        mass = wa + wb
        return top + jnp.log(mass), (wa * a[1] + wb * b[1]) / mass

    key_lane = lax.broadcasted_iota(jnp.int32, (1, pad), 1)
    own_bias = jnp.where(key_lane < rows, 0.0, NEG)
    fresh = []
    for p in range(pairs):
        cut = slice(p * PAIR, (p + 1) * PAIR)
        fresh.append(attend(queries[:, cut], keys[:, cut], values[:, cut], [own_bias]))

    def pass_on(buf, send, recv):
        for k in range(1, lines):
            copy = core_copy(buf, chip_at(k) * CORES + core, send, recv)
            copy.wait_recv()
            copy.start()

    def take(buf, send, recv):
        for k in range(lines):
            core_copy(buf, chip_at(k) * CORES + 1 - core, send, recv).wait_recv()

    pass_on(kv, core_send, kv_recv)

    @pl.when(is_host)
    def _():
        pass_on(kx, corex_send, kx_recv)

    take(kv, core_send, kv_recv)
    for k in range(1, WAYS):
        way_wait(k, qb, q_send, q_recv).wait_recv()

    step = n // blocks
    span = step * pad
    position = lax.broadcasted_iota(jnp.int32, (1, span), 1)
    padding = jnp.where(lax.rem(position, pad) < rows, 0.0, NEG)

    def bias_for(owner, b):
        start = (owner - b * step) * pad
        return jnp.where((position >= start) & (position < start + pad), NEG, padding)

    owners = [(block * WAYS + w) * CORES + core for w in range(WAYS)]

    def stale_part(packed, buf, dst):
        folds = packed[...].reshape(WAYS * fold, PAIR).astype(F32)
        query = jnp.concatenate(
            [jnp.where(half, folds, 0.0), jnp.where(half, swap(folds), 0.0)], axis=0
        ).astype(BF16)

        def one(b):
            pair = buf[pl.ds(b * step, step)].reshape(span, PAIR)
            biases = [bias_for(o, b) for o in owners]
            return one_head(query, pair, pair, biases + biases, fold)

        state = one(0)
        if blocks > 1:
            state = lax.fori_loop(1, blocks, lambda b, s: merge(s, one(b)), state)
        lse, part = state
        low, high = part[:WAYS * fold], part[WAYS * fold:]
        part = jnp.where(half, swap(high), low)
        lse = jnp.where(half, lse[WAYS * fold:], lse[:WAYS * fold])
        none = jnp.zeros((1, PAIR), F32)
        for w in range(WAYS):
            cut = slice(w * fold, (w + 1) * fold)
            flat = jnp.transpose(
                jnp.concatenate([lse[cut], jnp.zeros((PAIR - fold, PAIR), F32)], axis=0)
            )
            stats = jnp.concatenate(
                [*thirds(flat[0:1]), *thirds(flat[PAIR // 2:PAIR // 2 + 1]), none, none], axis=0
            )
            body = part[cut]
            end = jnp.where(half, stats, body[fold - 8:])
            dst[w] = jnp.concatenate([body[:fold - 8], end], axis=0).astype(BF16)

    stale_part(qb, kv, og)
    for k in range(1, WAYS):
        way_copy(k, og, ob, o_send, o_recv).start()
    ob[way] = og[way]

    @pl.when(is_host)
    def _():
        take(kx, corex_send, kx_recv)
        for k in range(1, WAYS):
            way_wait(k, qx, ox_send, qx_recv).wait_recv()
        stale_part(qx, kx, ox)
        for k in range(1, WAYS):
            host_result(k).start()
        ob[extra] = ox[way]

    def unfold(h):
        got = ob[h].astype(F32)
        stats = got[fold - 8:]
        high = stats[0:1] + stats[1:2] + stats[2:3]
        low = stats[3:4] + stats[4:5] + stats[5:6]
        lse = jnp.transpose(
            jnp.concatenate(
                [jnp.broadcast_to(high, (PAIR // 2, PAIR)), jnp.broadcast_to(low, (PAIR // 2, PAIR))],
                axis=0,
            )
        )[:fold]
        both = []
        for a in (lse, got):
            order = [swap(a), a] if h % 2 == 0 else [a, swap(a)]
            both.append(jnp.concatenate(order, axis=0))
        return both

    for k in range(1, WAYS):
        way_wait(k, ob, o_send, o_recv).wait_recv()
    heads = []
    for p in range(pairs):
        if p == WAYS // 2:
            for e in range(2):
                @pl.when(way != HOSTS[e])
                def _():
                    host_result_wait(e).wait_recv()
        even, odd = unfold(2 * p), unfold(2 * p + 1)
        stale = (jnp.where(half, even[0], odd[0]), jnp.where(half, even[1], odd[1]))
        heads.append(merge(fresh[p], stale)[1].astype(BF16))
    attended = jnp.concatenate(heads, axis=1)
    out_copy.wait()
    result = jnp.dot(attended, wo[...], preferred_element_type=F32) + bias_ref[...][None]
    out_ref[...] = result.astype(BF16)[:rows]

    for i in range(n - 1):
        mom_copy(i).wait_send()
    for e in range(2):
        for b in range(blocks):
            @pl.when(chip != b * WAYS + HOSTS[e])
            def _():
                host_copy(e, b).wait_send()

        @pl.when(way != HOSTS[e])
        def _():
            host_query(e).wait_send()
    for k in range(1, lines):
        line_copy(k).wait_send()
    for k in range(lines):
        core_copy(kv, chip_at(k) * CORES + core, core_send, kv_recv).wait_send()
    for k in range(1, WAYS):
        way_copy(k, qs, qb, q_send, q_recv).wait_send()
        way_copy(k, og, ob, o_send, o_recv).wait_send()

    @pl.when(is_host)
    def _():
        for k in range(lines):
            core_copy(kx, chip_at(k) * CORES + core, corex_send, kx_recv).wait_send()
        for k in range(1, WAYS):
            host_result(k).wait_send()


def solution(mesh):
    n = mesh.shape["patch"]

    def local(latents, stale_kv, stale_moments, norm_gain, norm_shift, w_qkv, w_out, out_bias):
        rows, width = latents.shape
        inner = w_out.shape[0]
        pad = -(-rows // 32) * 32
        heads = inner * 2 // PAIR
        chips = n // CORES
        vmem = pl.BlockSpec(memory_space=pltpu.VMEM)
        hbm = pl.BlockSpec(memory_space=pltpu.HBM)
        dma = pltpu.SemaphoreType.DMA
        return pl.pallas_call(
            functools.partial(kernel, n, rows, pad),
            out_shape=(
                jax.ShapeDtypeStruct((rows, w_out.shape[1]), BF16),
                jax.ShapeDtypeStruct((rows, 2 * inner), BF16),
            ),
            in_specs=[hbm] * 8,
            out_specs=(vmem, vmem),
            scratch_shapes=[
                pltpu.VMEM(latents.shape, BF16),
                pltpu.VMEM(stale_kv.shape, BF16),
                pltpu.VMEM(stale_moments.shape, F32),
                pltpu.VMEM(norm_gain.shape, F32),
                pltpu.VMEM(norm_shift.shape, F32),
                pltpu.VMEM(out_bias.shape, F32),
                pltpu.VMEM((heads, pad, PAIR), BF16),
                pltpu.VMEM((n, pad, PAIR), BF16),
                pltpu.VMEM((n, pad, PAIR), BF16),
                pltpu.VMEM((n, 8, stale_moments.shape[1]), F32),
                pltpu.VMEM((heads, pad // 2, PAIR), BF16),
                pltpu.VMEM((WAYS, pad // 2, PAIR), BF16),
                pltpu.VMEM((WAYS, pad // 2, PAIR), BF16),
                pltpu.VMEM((heads, pad // 2, PAIR), BF16),
                pltpu.VMEM((WAYS, pad // 2, PAIR), BF16),
                pltpu.VMEM((WAYS, pad // 2, PAIR), BF16),
                pltpu.VMEM((3, width, inner), BF16),
                pltpu.VMEM(w_out.shape, BF16),
                dma((n,)), dma((n,)), dma((chips,)), dma((n,)), dma((2 * chips // WAYS,)),
                dma((n,)), dma((n,)), dma((n,)),
                dma((WAYS,)), dma((WAYS,)), dma((2,)), dma((WAYS,)),
                dma((WAYS,)), dma((heads,)), dma((WAYS,)), dma((4,)), dma((6,)),
            ],
            compiler_params=pltpu.CompilerParams(
                collective_id=0, has_side_effects=True, vmem_limit_bytes=63 * 1024 * 1024
            ),
        )(
            latents, stale_kv, stale_moments, norm_gain, norm_shift, w_qkv, w_out, out_bias,
        )

    strip = P(("groups", "patch"), None)
    return jax.shard_map(
        local,
        mesh=mesh,
        in_specs=(strip, strip, strip, P(), P(), P(), P(), P()),
        out_specs=(strip, strip),
        check_vma=False,
    )
```

```python
import functools

import jax
import jax.numpy as jnp
from jax import lax
from jax.experimental import pallas as pl
from jax.experimental.pallas import tpu as pltpu
from jax.sharding import PartitionSpec as P

MESH = pl.DeviceIdType.MESH
PAIR = 128
CORES = 2
WAYS = 8
HOSTS = (2, 5)
NEG = -1e30
F32 = jnp.float32
BF16 = jnp.bfloat16


def dot_t(a, b):
    return lax.dot_general(a, b, (((1,), (1,)), ((), ())), preferred_element_type=F32)


def thirds(row):
    high = row.astype(BF16).astype(F32)
    rest = row - high
    mid = rest.astype(BF16).astype(F32)
    return high, mid, rest - mid


def kernel(
    n, rows, pad,
    x_hbm, stale_hbm, mom_hbm, gain_hbm, shift_hbm, wqkv_ref, wout_ref, bias_hbm,
    out_ref, fresh_ref,
    x_ref, stale_ref, mom_ref, gain_ref, shift_ref, bias_ref,
    sb, kv, kx, momb, qs, qb, qx, ob, og, ox, wq, wo,
    mom_send, mom_recv, kv_send, kv_recv, kx_send, kx_recv, core_send, corex_send,
    q_send, q_recv, qx_send, qx_recv, o_send, o_recv, ox_send, w_sem, in_sem,
):
    width = x_ref.shape[1]
    inner = stale_ref.shape[1] // 2
    me = lax.axis_index("patch")
    core = lax.rem(me, CORES)
    chip = me // CORES
    way = lax.rem(chip, WAYS)
    block = chip // WAYS
    lines = n // CORES
    blocks = lines // WAYS
    fold = pad // 2
    half = lax.broadcasted_iota(jnp.int32, (1, PAIR), 1) < PAIR // 2
    is_host = (way == HOSTS[0]) | (way == HOSTS[1])
    extra = jnp.where(way == HOSTS[1], WAYS + 1, WAYS)

    def swap(a):
        return pltpu.roll(a, PAIR // 2, 1)

    ins = [
        pltpu.make_async_copy(src, dst, in_sem.at[i])
        for i, (src, dst) in enumerate([
            (stale_hbm, stale_ref), (mom_hbm, mom_ref), (x_hbm, x_ref),
            (gain_hbm, gain_ref), (shift_hbm, shift_ref), (bias_hbm, bias_ref),
        ])
    ]
    for copy in ins:
        copy.start()
    weight_copies = [
        pltpu.make_async_copy(
            wqkv_ref.at[:, pl.ds(i * inner, inner)], wq.at[i], w_sem.at[i]
        )
        for i in range(3)
    ]
    out_copy = pltpu.make_async_copy(wout_ref, wo, w_sem.at[3])
    for copy in weight_copies:
        copy.start()
    out_copy.start()

    barrier = pltpu.get_barrier_semaphore()

    def greet(i, carry):
        pl.semaphore_signal(
            barrier, inc=1, device_id={"patch": lax.rem(me + 1 + i, n)}, device_id_type=MESH
        )
        return carry

    lax.fori_loop(0, n - 1, greet, 0, unroll=True)

    ins[0].wait()
    ins[1].wait()

    momb[me] = jnp.broadcast_to(mom_ref[...], (8, mom_ref.shape[1]))
    tail = jnp.zeros((pad - rows, PAIR), F32)

    def piece(c):
        part = stale_ref[:, c * PAIR:(c + 1) * PAIR].astype(F32)
        return jnp.concatenate([part, tail], axis=0)

    pairs = inner // PAIR
    for p in range(pairs):
        key, value = piece(p), piece(pairs + p)
        sb[2 * p] = jnp.where(half, key, swap(value)).astype(BF16)
        sb[2 * p + 1] = jnp.where(half, swap(key), value).astype(BF16)
    kv[me] = sb[way]

    @pl.when(is_host)
    def _():
        kx[me] = sb[extra]

    pl.semaphore_wait(barrier, n - 1)

    def mom_copy(i):
        peer = lax.rem(me + 1 + i, n)
        return pltpu.make_async_remote_copy(
            src_ref=momb.at[me], dst_ref=momb.at[me],
            send_sem=mom_send.at[i], recv_sem=mom_recv.at[me],
            device_id={"patch": peer}, device_id_type=MESH,
        )

    def mom_wait(i):
        peer = lax.rem(me + 1 + i, n)
        return pltpu.make_async_remote_copy(
            src_ref=momb.at[peer], dst_ref=momb.at[peer],
            send_sem=mom_send.at[i], recv_sem=mom_recv.at[peer],
            device_id={"patch": peer}, device_id_type=MESH,
        )

    def chip_at(k):
        return lax.rem(chip + k, lines)

    def line_copy(k):
        peer = chip_at(k)
        return pltpu.make_async_remote_copy(
            src_ref=sb.at[lax.rem(peer, WAYS)], dst_ref=kv.at[me],
            send_sem=kv_send.at[k], recv_sem=kv_recv.at[me],
            device_id={"patch": peer * CORES + core}, device_id_type=MESH,
        )

    def host_copy(e, b):
        peer = b * WAYS + HOSTS[e]
        return pltpu.make_async_remote_copy(
            src_ref=sb.at[WAYS + e], dst_ref=kx.at[me],
            send_sem=kx_send.at[e * blocks + b], recv_sem=kx_recv.at[me],
            device_id={"patch": peer * CORES + core}, device_id_type=MESH,
        )

    def core_copy(buf, slot, send, recv):
        return pltpu.make_async_remote_copy(
            src_ref=buf.at[slot], dst_ref=buf.at[slot],
            send_sem=send.at[slot], recv_sem=recv.at[slot],
            device_id={"patch": chip * CORES + 1 - core}, device_id_type=MESH,
        )

    def block_peer(w):
        return {"patch": (block * WAYS + w) * CORES + core}

    def way_copy(k, src, dst, send, recv):
        peer = lax.rem(way + k, WAYS)
        return pltpu.make_async_remote_copy(
            src_ref=src.at[peer], dst_ref=dst.at[way],
            send_sem=send.at[k], recv_sem=recv.at[way],
            device_id=block_peer(peer), device_id_type=MESH,
        )

    def way_wait(k, dst, send, recv):
        peer = lax.rem(way + k, WAYS)
        return pltpu.make_async_remote_copy(
            src_ref=dst.at[peer], dst_ref=dst.at[peer],
            send_sem=send.at[k], recv_sem=recv.at[peer],
            device_id=block_peer(peer), device_id_type=MESH,
        )

    def host_query(e):
        return pltpu.make_async_remote_copy(
            src_ref=qs.at[WAYS + e], dst_ref=qx.at[way],
            send_sem=qx_send.at[e], recv_sem=qx_recv.at[way],
            device_id=block_peer(HOSTS[e]), device_id_type=MESH,
        )

    def host_result(k):
        peer = lax.rem(way + k, WAYS)
        return pltpu.make_async_remote_copy(
            src_ref=ox.at[peer], dst_ref=ob.at[extra],
            send_sem=ox_send.at[k], recv_sem=o_recv.at[extra],
            device_id=block_peer(peer), device_id_type=MESH,
        )

    def host_result_wait(e):
        return pltpu.make_async_remote_copy(
            src_ref=ob.at[WAYS + e], dst_ref=ob.at[WAYS + e],
            send_sem=ox_send.at[0], recv_sem=o_recv.at[WAYS + e],
            device_id=block_peer(HOSTS[e]), device_id_type=MESH,
        )

    for i in range(n - 1):
        mom_copy(i).start()
    for e in range(2):
        for b in range(blocks):
            @pl.when(chip != b * WAYS + HOSTS[e])
            def _():
                host_copy(e, b).start()
    for k in range(1, lines):
        line_copy(k).start()
    core_copy(kv, me, core_send, kv_recv).start()

    @pl.when(is_host)
    def _():
        core_copy(kx, me, corex_send, kx_recv).start()

    count = mom_ref.shape[1]
    groups = count // 2
    size = width // groups
    for copy in ins[2:]:
        copy.wait()
    x = x_ref[...].astype(F32)
    first = jnp.sum(x, axis=0, keepdims=True)
    second = jnp.sum(x * x, axis=0, keepdims=True)
    lane = lax.broadcasted_iota(jnp.int32, (PAIR, width), 1)
    low = lax.rem(lax.broadcasted_iota(jnp.int32, (PAIR, width), 0), groups) * size
    member = jnp.where((lane >= low) & (lane < low + size), 1.0, 0.0).astype(BF16)
    zero = jnp.zeros((1, width), F32)
    table = jnp.concatenate([*thirds(first), *thirds(second), zero, zero], axis=0)
    sums = dot_t(table.astype(BF16), member)
    head = lax.broadcasted_iota(jnp.int32, (1, PAIR), 1)
    fresh_moments = jnp.where(
        head < groups, sums[0:1] + sums[1:2] + sums[2:3], sums[3:4] + sums[4:5] + sums[5:6]
    )
    stale_sum = jnp.zeros((8, count), F32)
    for i in range(n - 1):
        mom_wait(i).wait_recv()
        stale_sum = stale_sum + momb[lax.rem(me + 1 + i, n)]
    stale_row = jnp.concatenate(
        [stale_sum[0:1], jnp.zeros((1, PAIR - count), F32)], axis=1
    )
    totals = fresh_moments + stale_row
    left = jnp.where(head < groups, totals, 0.0)
    right = jnp.where((head >= groups) & (head < count), totals, 0.0)
    none = jnp.zeros((1, PAIR), F32)
    table = jnp.concatenate([*thirds(left), *thirds(right), none, none], axis=0)
    spreadout = jnp.dot(table.astype(BF16), member, preferred_element_type=F32)
    element_count = float(n * rows * size)
    mean = (spreadout[0:1] + spreadout[1:2] + spreadout[2:3]) / element_count
    spread = (spreadout[3:4] + spreadout[4:5] + spreadout[5:6]) / element_count - mean * mean
    inverse = lax.rsqrt(spread + 1e-06)
    normed = ((x - mean) * inverse) * gain_ref[...][None] + shift_ref[...][None]
    normed = jnp.concatenate([normed, jnp.zeros((pad - rows, width), F32)], axis=0).astype(BF16)

    weight_copies[0].wait()
    queries = jnp.dot(normed, wq[0], preferred_element_type=F32).astype(BF16)
    queries = (queries.astype(F32) * 0.125).astype(BF16)
    def folded(a):
        return jnp.where(half, a[:fold], swap(a[fold:]))

    for p in range(pairs):
        query = queries[:, p * PAIR:(p + 1) * PAIR].astype(F32)
        qs[2 * p] = folded(query).astype(BF16)
        qs[2 * p + 1] = folded(swap(query)).astype(BF16)
    qb[way] = qs[way]
    for k in range(1, WAYS):
        way_copy(k, qs, qb, q_send, q_recv).start()
    for e in range(2):
        @pl.when(way == HOSTS[e])
        def _():
            qx[way] = qs[WAYS + e]

        @pl.when(way != HOSTS[e])
        def _():
            host_query(e).start()

    weight_copies[1].wait()
    keys = jnp.dot(normed, wq[1], preferred_element_type=F32).astype(BF16)
    fresh_ref[:, :inner] = keys[:rows]
    weight_copies[2].wait()
    values = jnp.dot(normed, wq[2], preferred_element_type=F32).astype(BF16)
    fresh_ref[:, inner:] = values[:rows]

    def one_head(query, key, value, biases, seg):
        scores = dot_t(query, key)
        if len(biases) == 1:
            scores = scores + biases[0]
        else:
            scores = jnp.concatenate(
                [scores[i * seg:(i + 1) * seg] + b for i, b in enumerate(biases)], axis=0
            )
        top = jnp.max(scores, axis=1, keepdims=True)
        chances = jnp.exp(scores - top)
        mass = jnp.sum(chances, axis=1, keepdims=True)
        weighted = jnp.dot(chances.astype(BF16), value, preferred_element_type=F32)
        return top + jnp.log(mass), weighted / mass

    def attend(query, key, value, biases):
        none = jnp.zeros_like(query)
        lse0, out0 = one_head(jnp.where(half, query, none), key, value, biases, pad)
        lse1, out1 = one_head(jnp.where(half, none, query), key, value, biases, pad)
        return jnp.where(half, lse0, lse1), jnp.where(half, out0, out1)

    def merge(a, b):
        top = jnp.maximum(a[0], b[0])
        wa = jnp.exp(a[0] - top)
        wb = jnp.exp(b[0] - top)
        mass = wa + wb
        return top + jnp.log(mass), (wa * a[1] + wb * b[1]) / mass

    def pass_on(buf, send, recv, steps):
        for k in steps:
            copy = core_copy(buf, chip_at(k) * CORES + core, send, recv)
            copy.wait_recv()
            copy.start()

    key_lane = lax.broadcasted_iota(jnp.int32, (1, pad), 1)
    own_bias = jnp.where(key_lane < rows, 0.0, NEG)
    fresh = []
    order = sorted(range(1, lines), key=lambda k: min(k, lines - k))
    share = -(-len(order) // pairs)
    for p in range(pairs):
        cut = slice(p * PAIR, (p + 1) * PAIR)
        fresh.append(attend(queries[:, cut], keys[:, cut], values[:, cut], [own_bias]))
        pass_on(kv, core_send, kv_recv, order[p * share:(p + 1) * share])

    def take(buf, send, recv):
        for k in range(lines):
            core_copy(buf, chip_at(k) * CORES + 1 - core, send, recv).wait_recv()

    @pl.when(is_host)
    def _():
        pass_on(kx, corex_send, kx_recv, range(1, lines))

    take(kv, core_send, kv_recv)
    for k in range(1, WAYS):
        way_wait(k, qb, q_send, q_recv).wait_recv()

    step = n // blocks
    span = step * pad
    position = lax.broadcasted_iota(jnp.int32, (1, span), 1)
    padding = jnp.where(lax.rem(position, pad) < rows, 0.0, NEG)

    def bias_for(owner, b):
        start = (owner - b * step) * pad
        return jnp.where((position >= start) & (position < start + pad), NEG, padding)

    owners = [(block * WAYS + w) * CORES + core for w in range(WAYS)]

    def stale_part(packed, buf, dst):
        folds = packed[...].reshape(WAYS * fold, PAIR).astype(F32)
        query = jnp.concatenate(
            [jnp.where(half, folds, 0.0), jnp.where(half, swap(folds), 0.0)], axis=0
        ).astype(BF16)

        def one(b):
            pair = buf[pl.ds(b * step, step)].reshape(span, PAIR)
            biases = [bias_for(o, b) for o in owners]
            return one_head(query, pair, pair, biases + biases, fold)

        state = one(0)
        if blocks > 1:
            state = lax.fori_loop(1, blocks, lambda b, s: merge(s, one(b)), state)
        lse, part = state
        low, high = part[:WAYS * fold], part[WAYS * fold:]
        part = jnp.where(half, swap(high), low)
        lse = jnp.where(half, lse[WAYS * fold:], lse[:WAYS * fold])
        none = jnp.zeros((1, PAIR), F32)
        for w in range(WAYS):
            cut = slice(w * fold, (w + 1) * fold)
            flat = jnp.transpose(
                jnp.concatenate([lse[cut], jnp.zeros((PAIR - fold, PAIR), F32)], axis=0)
            )
            stats = jnp.concatenate(
                [*thirds(flat[0:1]), *thirds(flat[PAIR // 2:PAIR // 2 + 1]), none, none], axis=0
            )
            body = part[cut]
            end = jnp.where(half, stats, body[fold - 8:])
            dst[w] = jnp.concatenate([body[:fold - 8], end], axis=0).astype(BF16)

    stale_part(qb, kv, og)
    for k in range(1, WAYS):
        way_copy(k, og, ob, o_send, o_recv).start()
    ob[way] = og[way]

    @pl.when(is_host)
    def _():
        take(kx, corex_send, kx_recv)
        for k in range(1, WAYS):
            way_wait(k, qx, ox_send, qx_recv).wait_recv()
        stale_part(qx, kx, ox)
        for k in range(1, WAYS):
            host_result(k).start()
        ob[extra] = ox[way]

    def unfold(h):
        got = ob[h].astype(F32)
        stats = got[fold - 8:]
        high = stats[0:1] + stats[1:2] + stats[2:3]
        low = stats[3:4] + stats[4:5] + stats[5:6]
        lse = jnp.transpose(
            jnp.concatenate(
                [jnp.broadcast_to(high, (PAIR // 2, PAIR)), jnp.broadcast_to(low, (PAIR // 2, PAIR))],
                axis=0,
            )
        )[:fold]
        both = []
        for a in (lse, got):
            order = [swap(a), a] if h % 2 == 0 else [a, swap(a)]
            both.append(jnp.concatenate(order, axis=0))
        return both

    for k in range(1, WAYS):
        way_wait(k, ob, o_send, o_recv).wait_recv()
    heads = []
    for p in range(pairs):
        if p == WAYS // 2:
            for e in range(2):
                @pl.when(way != HOSTS[e])
                def _():
                    host_result_wait(e).wait_recv()
        even, odd = unfold(2 * p), unfold(2 * p + 1)
        stale = (jnp.where(half, even[0], odd[0]), jnp.where(half, even[1], odd[1]))
        heads.append(merge(fresh[p], stale)[1].astype(BF16))
    attended = jnp.concatenate(heads, axis=1)
    out_copy.wait()
    result = jnp.dot(attended, wo[...], preferred_element_type=F32) + bias_ref[...][None]
    out_ref[...] = result.astype(BF16)[:rows]

    for i in range(n - 1):
        mom_copy(i).wait_send()
    for e in range(2):
        for b in range(blocks):
            @pl.when(chip != b * WAYS + HOSTS[e])
            def _():
                host_copy(e, b).wait_send()

        @pl.when(way != HOSTS[e])
        def _():
            host_query(e).wait_send()
    for k in range(1, lines):
        line_copy(k).wait_send()
    for k in range(lines):
        core_copy(kv, chip_at(k) * CORES + core, core_send, kv_recv).wait_send()
    for k in range(1, WAYS):
        way_copy(k, qs, qb, q_send, q_recv).wait_send()
        way_copy(k, og, ob, o_send, o_recv).wait_send()

    @pl.when(is_host)
    def _():
        for k in range(lines):
            core_copy(kx, chip_at(k) * CORES + core, corex_send, kx_recv).wait_send()
        for k in range(1, WAYS):
            host_result(k).wait_send()


def solution(mesh):
    n = mesh.shape["patch"]

    def local(latents, stale_kv, stale_moments, norm_gain, norm_shift, w_qkv, w_out, out_bias):
        rows, width = latents.shape
        inner = w_out.shape[0]
        pad = -(-rows // 32) * 32
        heads = inner * 2 // PAIR
        chips = n // CORES
        vmem = pl.BlockSpec(memory_space=pltpu.VMEM)
        hbm = pl.BlockSpec(memory_space=pltpu.HBM)
        dma = pltpu.SemaphoreType.DMA
        return pl.pallas_call(
            functools.partial(kernel, n, rows, pad),
            out_shape=(
                jax.ShapeDtypeStruct((rows, w_out.shape[1]), BF16),
                jax.ShapeDtypeStruct((rows, 2 * inner), BF16),
            ),
            in_specs=[hbm] * 8,
            out_specs=(vmem, vmem),
            scratch_shapes=[
                pltpu.VMEM(latents.shape, BF16),
                pltpu.VMEM(stale_kv.shape, BF16),
                pltpu.VMEM(stale_moments.shape, F32),
                pltpu.VMEM(norm_gain.shape, F32),
                pltpu.VMEM(norm_shift.shape, F32),
                pltpu.VMEM(out_bias.shape, F32),
                pltpu.VMEM((heads, pad, PAIR), BF16),
                pltpu.VMEM((n, pad, PAIR), BF16),
                pltpu.VMEM((n, pad, PAIR), BF16),
                pltpu.VMEM((n, 8, stale_moments.shape[1]), F32),
                pltpu.VMEM((heads, pad // 2, PAIR), BF16),
                pltpu.VMEM((WAYS, pad // 2, PAIR), BF16),
                pltpu.VMEM((WAYS, pad // 2, PAIR), BF16),
                pltpu.VMEM((heads, pad // 2, PAIR), BF16),
                pltpu.VMEM((WAYS, pad // 2, PAIR), BF16),
                pltpu.VMEM((WAYS, pad // 2, PAIR), BF16),
                pltpu.VMEM((3, width, inner), BF16),
                pltpu.VMEM(w_out.shape, BF16),
                dma((n,)), dma((n,)), dma((chips,)), dma((n,)), dma((2 * chips // WAYS,)),
                dma((n,)), dma((n,)), dma((n,)),
                dma((WAYS,)), dma((WAYS,)), dma((2,)), dma((WAYS,)),
                dma((WAYS,)), dma((heads,)), dma((WAYS,)), dma((4,)), dma((6,)),
            ],
            compiler_params=pltpu.CompilerParams(
                collective_id=0, has_side_effects=True, vmem_limit_bytes=63 * 1024 * 1024
            ),
        )(
            latents, stale_kv, stale_moments, norm_gain, norm_shift, w_qkv, w_out, out_bias,
        )

    strip = P(("groups", "patch"), None)
    return jax.shard_map(
        local,
        mesh=mesh,
        in_specs=(strip, strip, strip, P(), P(), P(), P(), P()),
        out_specs=(strip, strip),
        check_vma=False,
    )
```
